256 devices in a mesh: chan: 32 (over y, z_hi, x), win: 8 (over z_lo, core).
Axes of the slice: x: 4, y: 4, z: 8 (z_hi: 2, z_lo: 4; z = z_hi * 4 + z_lo), core: 2. Of those that a mesh axis runs over, the one named last changes fastest.
Arguments:
- spectra: bfloat16 [8, 4096, 2, 2048], P('win', 'chan'), may hold values from -400 to 400
- pair_first: int32 [32, 1024], P('chan'), may hold values from 0 to 127
- pair_second: int32 [32, 1024], P('chan'), may hold values from 0 to 511, as said below
- pair_count: int32 [32], P('chan'), may hold values from 128 to 1024, as said below
- pair_owner: int32 [32, 1024, 1], P('chan'), may hold values from 0 to 31; in each aligned block of 1024 rows (0 to 1023, 1024 to 2047, ..., all dimensions but the last counted through in order) at most 64 rows name the same one
Outputs:
- stacks: float32 [32, 32, 64, 512], P('chan', None, None, 'win')
The draws below stay inside these ranges and needn't reach their ends.
Inputs may be any that keep to these rules, and one draw needn't show every extreme that they name: pair_second[b, s] lies between pair_first[b, s] and pair_first[b, s] + 384, and b * 128 + pair_second[b, s] is below 4096. `pair_count`: some block has 1024 listed pairs. `pair_owner`: among the 1024 slots of one block no owner is named more than 64 times.
All inputs are finite; a program needn't handle non-finite values.
Results may differ from the reference program's by a relative error of at most 0.017.
Values may be sent and summed in bfloat16 or wider, within the bound.
No kernel may reach another device: no remote copies, remote signals or barrier semaphores. Data moves between devices by JAX's collectives and lax.ppermute only.
A program may use at most 128 MiB of HBM per device.

```python
import math
import jax
import jax.numpy as jnp
import numpy as np
from jax import lax

CH_DEV = 128
F = 2048
LAGS = 512
REACH = 3
PAIR_CAP = 1024
BLOCKS = 32
CHANNELS = 4096
WINDOWS = 8
MOST = 64
N_CHAN = 32


def pair_lists(key):
    key_first, key_gap = jax.random.split(key)
    first_local = jax.random.randint(key_first, (BLOCKS, PAIR_CAP), 0, CH_DEV, dtype=jnp.int32)
    raw_gap = jax.random.randint(key_gap, (BLOCKS, PAIR_CAP), 0, REACH * CH_DEV + 1, dtype=jnp.int32)
    global_first = jnp.arange(BLOCKS, dtype=jnp.int32)[:, None] * CH_DEV + first_local
    room_left = jnp.minimum(REACH * CH_DEV, CHANNELS - 1 - global_first)
    gap_size = raw_gap % (room_left + 1)
    second_local = first_local + gap_size
    first_local = first_local.at[0, 0].set(CH_DEV - 1)
    second_local = second_local.at[0, 0].set((REACH + 1) * CH_DEV - 1)
    return (first_local, second_local)


def draw_pair_first(key, part):
    shared = pair_lists(key)
    return shared[0]


def draw_pair_second(key, part):
    shared = pair_lists(key)
    return shared[1]


def draw_pair_count(key, part):
    key = jax.random.fold_in(key, 5)
    key_counts, key_busy = jax.random.split(key)
    counts = jax.random.randint(key_counts, (BLOCKS,), PAIR_CAP // 8, PAIR_CAP // 3 + 1, dtype=jnp.int32)
    busiest = jax.random.randint(key_busy, (), 0, BLOCKS, dtype=jnp.int32)
    return counts.at[busiest].set(PAIR_CAP)


def draw_spectra(key, part):
    key = jax.random.fold_in(key, 11)
    key_noise, key_chan, key_bins = jax.random.split(key, 3)
    shape = (WINDOWS, CHANNELS, 2, F)
    chan_scale = jnp.exp(jax.random.uniform(key_chan, (WINDOWS, CHANNELS, 1, 1), jnp.float32, 0.0, math.log(10.0)))
    bin_scale = jnp.exp(jax.random.uniform(key_bins, (1, 1, 1, F), jnp.float32, 0.0, math.log(10.0)))
    base_noise = jnp.clip(jax.random.normal(key_noise, shape, jnp.float32), -4.0, 4.0)
    return (base_noise * chan_scale * bin_scale).astype(jnp.bfloat16)


def routed_block(rng, own, number, rows, number_of, top, bound, skew):
    sequence = jax.random.permutation(rng, number_of)
    packed, usual = load_shares(number_of, rows * top, bound, skew, True), load_shares(number_of, rows * top, bound, skew, False)
    places = jnp.arange(number_of)

    def named(tallies, rotation):
        used = int((tallies > 0).sum())
        fixed = max(1, used // 4)
        shifted = fixed + (places - fixed + rotation * (used - fixed)) % max(1, number_of - fixed)
        return jnp.zeros((number_of,), jnp.int32).at[sequence[jnp.where(places < fixed, places, shifted)]].set(jnp.asarray(tallies, jnp.int32))

    tallies = jnp.where(number % 4 == 0, named(packed, number // 4), named(usual, number - number // 4 - 1))
    mixed = jax.random.permutation(jax.random.fold_in(own, 3), number_of)
    donor, taker = mixed[0:number_of // 2 * 2:2], mixed[1:number_of // 2 * 2:2]
    slack = jnp.minimum(tallies[donor] - 1, bound - tallies[taker]) // 2
    slack = jnp.where((donor == sequence[0]) | (taker == sequence[0]) | (tallies[taker] == 0), 0, jnp.maximum(slack, 0))
    shifted = jax.random.randint(jax.random.fold_in(own, 4), (number_of // 2,), 0, 1 << 20) % (slack + 1)
    tallies = tallies.at[donor].add(-shifted).at[taker].add(shifted)
    items = jnp.searchsorted(jnp.cumsum(tallies), jnp.arange(rows * top), side="right").astype(jnp.int32)
    table = items.reshape(top, rows).T
    table = table[jax.random.permutation(jax.random.fold_in(own, 1), rows)]
    rotation = jax.random.randint(jax.random.fold_in(own, 2), (rows, 1), 0, top)
    return jnp.take_along_axis(table, (jnp.arange(top)[None, :] + rotation) % top, axis=1)


def load_shares(amount, total, most, slope, full):
    weights = [(1 << 20) // math.isqrt(rank ** slope) + 1 for rank in range(1, amount + 1)]
    largest = most if full else min(most, max(-(-total // amount), total * weights[0] // sum(weights)))
    least = 1 if total - largest >= amount - 1 else 0
    holding, spare = [largest] + [least] * (amount - 1), total - largest - least * (amount - 1)
    while spare > 0:
        movable = [i for i in range(1, amount) if holding[i] < largest] or [i for i in range(1, amount) if holding[i] < most]
        mass, left = sum([weights[i] for i in movable]), spare
        for i in movable:
            more = min(most - holding[i], max(1, left * weights[i] // mass), spare)
            holding[i] = holding[i] + more
            spare = spare - more
    return np.array(holding)


def setup_inputs(seed: int = 0) -> dict:
    seeds = jax.random.split(jax.random.key(seed), 6)
    spectra = draw_spectra(jax.random.fold_in(seeds[5], 71), 0)
    pair_first = draw_pair_first(jax.random.fold_in(seeds[5], 71), 0)
    pair_second = draw_pair_second(jax.random.fold_in(seeds[5], 71), 0)
    pair_count = draw_pair_count(jax.random.fold_in(seeds[5], 71), 0)
    pair_owner_keys = jax.random.split(jax.random.fold_in(seeds[4], 1), BLOCKS * PAIR_CAP // PAIR_CAP)
    pair_owner_turns = jax.random.permutation(jax.random.fold_in(seeds[4], 3), BLOCKS * PAIR_CAP // PAIR_CAP)
    pair_owner = jax.vmap(lambda own, number: routed_block(jax.random.fold_in(seeds[4], 2), own, number, PAIR_CAP, N_CHAN, 1, MOST, 2))(pair_owner_keys, pair_owner_turns).reshape((BLOCKS, PAIR_CAP, 1))
    return dict(spectra=spectra, pair_first=pair_first, pair_second=pair_second, pair_count=pair_count, pair_owner=pair_owner)


def lag_table(bins, lags, windows):
    freq_index = jnp.arange(bins, dtype=jnp.int32)
    lag_offset = jnp.arange(lags, dtype=jnp.int32) - lags // 2
    phase_index = freq_index[:, None] * lag_offset[None, :] % (2 * bins)
    angles = phase_index.astype(jnp.float32) * (math.pi / bins)
    weights = jnp.where(freq_index == 0, 1.0, 2.0).astype(jnp.float32)[:, None] / math.sqrt(bins * windows)
    return jnp.concatenate([weights * jnp.cos(angles), -weights * jnp.sin(angles)], 0).astype(jnp.bfloat16)

def whiten(spectra):
    values = spectra.astype(jnp.float32)
    power = lax.optimization_barrier(jnp.mean(values * values, axis=(2, 3), keepdims=True))
    return (values * lax.rsqrt(power + 1e-06)).astype(jnp.bfloat16)

def route(stacked, owners, blocks_total, capacity):
    onehot = (owners[:, None] == jnp.arange(blocks_total, dtype=jnp.int32)[None, :]).astype(jnp.int32)
    before = jnp.cumsum(onehot, axis=0, dtype=jnp.int32) - onehot
    position = lax.optimization_barrier(jnp.sum(before * onehot, axis=1)).astype(jnp.int32)
    buffer = jnp.zeros((blocks_total, capacity, stacked.shape[1]), jnp.float32)
    return buffer.at[owners, position].set(stacked)

def reference(spectra, pair_first, pair_second, pair_count, pair_owner):
    whitened = whiten(spectra)
    padded = jnp.pad(whitened, ((0, 0), (0, REACH * CH_DEV), (0, 0), (0, 0)))
    inverse = lag_table(F, LAGS, WINDOWS).astype(jnp.float32)
    slot_index = jnp.arange(PAIR_CAP, dtype=jnp.int32)

    def per_block(block_index):
        window = lax.dynamic_slice_in_dim(padded, block_index * CH_DEV, (REACH + 1) * CH_DEV, 1)
        left_rows = jnp.take(window, pair_first[block_index], axis=1).astype(jnp.float32)
        right_rows = jnp.take(window, pair_second[block_index], axis=1).astype(jnp.float32)
        real_part = left_rows[:, :, 0] * right_rows[:, :, 0] + left_rows[:, :, 1] * right_rows[:, :, 1]
        imag_part = left_rows[:, :, 1] * right_rows[:, :, 0] - left_rows[:, :, 0] * right_rows[:, :, 1]
        cross_spec = jnp.concatenate([real_part, imag_part], -1).astype(jnp.bfloat16)
        stacked = jnp.einsum('wpf,fl->pl', cross_spec.astype(jnp.float32), inverse)
        live = (slot_index < pair_count[block_index]).astype(jnp.float32)
        stacked = stacked * live[:, None]
        return route(stacked, pair_owner[block_index, :, 0], BLOCKS, MOST)
    buffers = lax.map(per_block, jnp.arange(BLOCKS, dtype=jnp.int32))
    return jnp.swapaxes(buffers, 0, 1)
```

```python
import functools
import math

import jax
import jax.numpy as jnp
from jax import lax
from jax.experimental import pallas as pl
from jax.experimental.pallas import tpu as pltpu
from jax.sharding import PartitionSpec as P

LAGS = 512
REACH = 3
CHUNKS = 4
ROWS = 256
AXES = ("chan", "win")
N_X = 4
N_CORE = 2


def pairs_of(move):
    pairs = []
    for chan in range(32):
        for win in range(8):
            row, x, z, core = chan // N_X, chan % N_X, win // N_CORE, win % N_CORE
            row, x, z, core = move(row, x, z, core)
            pairs.append((chan * 8 + win, (row * N_X + x) * 8 + z * N_CORE + core))
    return pairs


def to_previous_row(row, x, z, core):
    return ((row - 1) % 8 if x < REACH else row), x, z, core


CROSS = pairs_of(to_previous_row)
AROUND = {d: pairs_of(lambda row, x, z, core, d=d: (row, (x - d) % N_X, z, core)) for d in (1, 2, 3)}
OTHER_CORE = pairs_of(lambda row, x, z, core: (row, x, z, 1 - core))
OTHER_CHIP = {k: pairs_of(lambda row, x, z, core, k=k: (row, x, z ^ k, core)) for k in (1, 2, 3)}


def lag_table(bins, windows):
    win = lax.axis_index("win")
    z, core = win // N_CORE, win % N_CORE
    column = jnp.arange(LAGS, dtype=jnp.int32)
    half, block, inner = column // 256, column // 64 % 4, column % 64
    lag = ((z ^ block) * N_CORE + (core ^ half)) * 64 + inner - LAGS // 2
    freq_index = jnp.arange(bins, dtype=jnp.int32)
    phase_index = freq_index[:, None] * lag[None, :] % (2 * bins)
    angles = phase_index.astype(jnp.float32) * (math.pi / bins)
    weights = jnp.where(freq_index == 0, 1.0, 2.0).astype(jnp.float32)[:, None] / math.sqrt(
        bins * windows
    )
    return jnp.stack([weights * jnp.cos(angles), -weights * jnp.sin(angles)], 0).astype(jnp.bfloat16)


def whiten(spectra):
    values = spectra.astype(jnp.float32)
    power = jnp.mean(values * values, axis=(1, 2), keepdims=True)
    return (values * lax.rsqrt(power + 1e-06)).astype(jnp.bfloat16)


def dot(a, b):
    return lax.dot_general(a, b, (((1,), (0,)), ((), ())), preferred_element_type=jnp.float32)


def correlate(bins, first_ref, second_ref, own_ref, one_ref, two_ref, three_ref, table_ref, acc):
    left_hot = first_ref[...]
    right_hot = second_ref[...]
    step = min(512, bins)
    for start in range(0, bins, step):
        at = pl.ds(start, step)
        left = [dot(left_hot, own_ref[part, :, at]) for part in range(2)]
        right = [
            dot(
                right_hot,
                jnp.concatenate(
                    [ref[part, :, at] for ref in (own_ref, one_ref, two_ref, three_ref)], 0
                ),
            )
            for part in range(2)
        ]
        real = (left[0] * right[0] + left[1] * right[1]).astype(jnp.bfloat16)
        imag = (left[1] * right[0] - left[0] * right[1]).astype(jnp.bfloat16)
        part = dot(real, table_ref[0, at, :]) + dot(imag, table_ref[1, at, :])
        acc = part if acc is None else acc + part
    return acc


def first_kernel(bins, first, second, own, one, two, three, table, out):
    out[...] = correlate(bins, first, second, own, one, two, three, table, None)


def next_kernel(bins, first, second, own, one, two, three, table, acc, out):
    out[...] = correlate(bins, first, second, own, one, two, three, table, acc[...])


def last_kernel(bins, first, second, own, one, two, three, table, acc, keep, send):
    total = correlate(bins, first, second, own, one, two, three, table, acc[...])
    keep[...] = total[:, :256]
    send[...] = total[:, 256:].astype(jnp.bfloat16)


def run_chunk(kernel, first_hot, second_hot, blocks, table, acc, outs):
    slots = first_hot.shape[0]
    bins = blocks[0].shape[2]

    def rows(width):
        return pl.BlockSpec((ROWS, width), lambda i: (i, 0))

    def whole(shape):
        return pl.BlockSpec(shape, lambda i: (0,) * len(shape))

    operands = [first_hot, second_hot, *blocks, table] + ([] if acc is None else [acc])
    in_specs = [rows(128), rows(512)] + [whole(b.shape) for b in blocks] + [whole(table.shape)]
    in_specs += [] if acc is None else [rows(512)]
    return pl.pallas_call(
        functools.partial(kernel, bins),
        grid=(slots // ROWS,),
        in_specs=in_specs,
        out_specs=[rows(o.shape[1]) for o in outs],
        out_shape=outs,
        compiler_params=pltpu.CompilerParams(vmem_limit_bytes=56 << 20),
        cost_estimate=pl.CostEstimate(
            flops=2 * slots * 2 * bins * (640 + 512), bytes_accessed=8 << 20, transcendentals=0
        ),
        name="correlate",
    )(*operands)


def split_kernel(keep, received, *outs):
    total = keep[...] + received[...].astype(jnp.float32)
    half = total.shape[0] // 2
    for k, out in enumerate(outs):
        piece = total[:, 64 * k : 64 * k + 64]
        out[...] = jnp.concatenate([piece[:half], piece[half:]], 1).astype(out.dtype)


def route_kernel(hot, keep, one, two, three, out):
    total = keep[...]
    for ref in (one, two, three):
        total = total + ref[...].astype(jnp.float32)
    rows = jnp.concatenate([total[:, :64], total[:, 64:]], 0).astype(jnp.bfloat16)
    for owner in range(32):
        placed = dot(hot[64 * owner : 64 * owner + 64, :], rows)
        out[owner] = jnp.concatenate([placed[:32], placed[32:]], 1).astype(jnp.bfloat16)


def unpack_kernel(routed, out):
    for block in range(32):
        values = routed[block].astype(jnp.float32)
        out[0, block, :32] = values[:, :64]
        out[0, block, 32:] = values[:, 64:]


def call(kernel, out_shape, *operands):
    return pl.pallas_call(
        kernel,
        out_shape=out_shape,
        compiler_params=pltpu.CompilerParams(vmem_limit_bytes=40 << 20),
        name=kernel.__name__,
    )(*operands)


def on_device(spectra, pair_first, pair_second, pair_count, pair_owner):
    windows_all = spectra.shape[0] * lax.axis_size("win")
    bins = spectra.shape[3]
    slots = pair_first.shape[1]
    x_place = lax.axis_index("chan") % N_X
    whitened = jnp.swapaxes(whiten(spectra[0]), 0, 1)
    size = bins // CHUNKS
    own = [whitened[:, :, q * size : (q + 1) * size] for q in range(CHUNKS)]
    crossed = [lax.ppermute(chunk, AXES, CROSS) for chunk in own]

    first_hot = (pair_first[0][:, None] == jnp.arange(128, dtype=jnp.int32)).astype(jnp.bfloat16)
    second_hot = (pair_second[0][:, None] == jnp.arange(512, dtype=jnp.int32)).astype(jnp.bfloat16)
    owners = pair_owner[0, :, 0]
    onehot = (owners[:, None] == jnp.arange(32, dtype=jnp.int32)[None, :]).astype(jnp.int32)
    before = jnp.cumsum(onehot, axis=0, dtype=jnp.int32) - onehot
    place = owners * 64 + jnp.sum(before * onehot, axis=1)
    place = jnp.where(jnp.arange(slots, dtype=jnp.int32) < pair_count[0], place, -1)
    place_hot = (place[None, :] == jnp.arange(2048, dtype=jnp.int32)[:, None]).astype(jnp.bfloat16)
    table = lag_table(bins, windows_all)

    acc = None
    f32 = jnp.float32
    for q in range(CHUNKS):
        ahead = {}
        for d in (2, 1, 3):
            source = jnp.where(x_place < d, crossed[q], own[q])
            ahead[d] = lax.ppermute(source, AXES, AROUND[d])
        blocks = [own[q], ahead[1], ahead[2], ahead[3]]
        part = table[:, q * size : (q + 1) * size]
        whole = jax.ShapeDtypeStruct((slots, LAGS), f32)
        if q == CHUNKS - 1:
            outs = [
                jax.ShapeDtypeStruct((slots, 256), f32),
                jax.ShapeDtypeStruct((slots, 256), jnp.bfloat16),
            ]
            keep, send = run_chunk(last_kernel, first_hot, second_hot, blocks, part, acc, outs)
        else:
            kernel = first_kernel if q == 0 else next_kernel
            (acc,) = run_chunk(kernel, first_hot, second_hot, blocks, part, acc, [whole])
    received = lax.ppermute(send, AXES, OTHER_CORE)
    packed = (slots // 2, 128)
    pieces = call(
        split_kernel,
        [jax.ShapeDtypeStruct(packed, f32)] + [jax.ShapeDtypeStruct(packed, jnp.bfloat16)] * 3,
        keep,
        received,
    )
    arrived = [lax.ppermute(pieces[k], AXES, OTHER_CHIP[k]) for k in (1, 2, 3)]
    buffer = call(
        route_kernel, jax.ShapeDtypeStruct((32, 32, 128), jnp.bfloat16), place_hot, pieces[0], *arrived
    )
    routed = lax.all_to_all(buffer, "chan", split_axis=0, concat_axis=0, tiled=True)
    return call(unpack_kernel, jax.ShapeDtypeStruct((1, 32, 64, 64), f32), routed)


def solution(mesh):
    in_specs = (
        P("win", "chan", None, None),
        P("chan", None),
        P("chan", None),
        P("chan"),
        P("chan", None, None),
    )
    out_specs = P("chan", None, None, "win")
    return jax.shard_map(
        on_device, mesh=mesh, in_specs=in_specs, out_specs=out_specs, check_vma=False
    )
```

```python
import functools
import math

import jax
import jax.numpy as jnp
from jax import lax
from jax.experimental import pallas as pl
from jax.experimental.pallas import tpu as pltpu
from jax.sharding import PartitionSpec as P

LAGS = 512
REACH = 3
CHUNKS = 4
FIRST_DONE = False
CHOOSE_COST = (5_000_000_000,) * 4
ROWS = 256
AXES = ("chan", "win")
N_X = 4
N_CORE = 2


def pairs_of(move):
    pairs = []
    for chan in range(32):
        for win in range(8):
            row, x, z, core = chan // N_X, chan % N_X, win // N_CORE, win % N_CORE
            row, x, z, core = move(row, x, z, core)
            pairs.append((chan * 8 + win, (row * N_X + x) * 8 + z * N_CORE + core))
    return pairs


def to_previous_row(row, x, z, core):
    return ((row - 1) % 8 if x < REACH else row), x, z, core


CROSS = pairs_of(to_previous_row)
AROUND = {d: pairs_of(lambda row, x, z, core, d=d: (row, (x - d) % N_X, z, core)) for d in (1, 2, 3)}
OTHER_CORE = pairs_of(lambda row, x, z, core: (row, x, z, 1 - core))
OTHER_CHIP = {k: pairs_of(lambda row, x, z, core, k=k: (row, x, z ^ k, core)) for k in (1, 2, 3)}


def lag_table(bins, windows):
    win = lax.axis_index("win")
    z, core = win // N_CORE, win % N_CORE
    column = jnp.arange(LAGS, dtype=jnp.int32)
    half, block, inner = column // 256, column // 64 % 4, column % 64
    lag = ((z ^ block) * N_CORE + (core ^ half)) * 64 + inner - LAGS // 2

    def turns(freq_index):
        phase_index = freq_index[:, None] * lag[None, :] % (2 * bins)
        angles = phase_index.astype(jnp.float32) * (math.pi / bins)
        return jnp.cos(angles), jnp.sin(angles)

    few = 32
    low_cos, low_sin = turns(jnp.arange(few, dtype=jnp.int32))
    high_cos, high_sin = turns(jnp.arange(0, bins, few, dtype=jnp.int32))
    low_cos, low_sin = low_cos[None], low_sin[None]
    high_cos, high_sin = high_cos[:, None], high_sin[:, None]
    weights = jnp.where(jnp.arange(bins, dtype=jnp.int32) == 0, 1.0, 2.0).astype(jnp.float32)
    weights = weights.reshape(bins // few, few, 1) / math.sqrt(bins * windows)
    cosine = weights * (high_cos * low_cos - high_sin * low_sin)
    sine = -weights * (high_sin * low_cos + high_cos * low_sin)
    return [part.astype(jnp.bfloat16).reshape(bins, LAGS) for part in (cosine, sine)]


def whiten(spectra):
    values = spectra.astype(jnp.float32)
    power = jnp.mean(values * values, axis=(1, 2), keepdims=True)
    return (values * lax.rsqrt(power + 1e-06)).astype(jnp.bfloat16)


def dot(a, b):
    return lax.dot_general(a, b, (((1,), (0,)), ((), ())), preferred_element_type=jnp.float32)


def correlate(first_ref, second_ref, halo, cos_ref, sin_ref, acc, blocks):
    @pl.when(pl.program_id(0) == 0)
    def _():
        for d, ref in enumerate(halo):
            blocks[:, 128 * d : 128 * (d + 1)] = ref[...]

    left_hot = first_ref[...]
    right_hot = second_ref[...]
    bins = blocks.shape[2]
    step = min(512, bins)
    for start in range(0, bins, step):
        at = pl.ds(start, step)
        left = [dot(left_hot, blocks[part, :128, at]) for part in range(2)]
        right = [dot(right_hot, blocks[part, :, at]) for part in range(2)]
        real = (left[0] * right[0] + left[1] * right[1]).astype(jnp.bfloat16)
        imag = (left[1] * right[0] - left[0] * right[1]).astype(jnp.bfloat16)
        part = dot(real, cos_ref[at, :]) + dot(imag, sin_ref[at, :])
        acc = part if acc is None else acc + part
    return acc


def first_kernel(first, second, *rest):
    *halo, cosine, sine, out, blocks = rest
    out[...] = correlate(first, second, halo, cosine, sine, None, blocks)


def next_kernel(first, second, *rest):
    *halo, cosine, sine, acc, out, blocks = rest
    out[...] = correlate(first, second, halo, cosine, sine, acc[...], blocks)


def last_kernel(first, second, *rest):
    *halo, cosine, sine, acc, keep, send, blocks = rest
    total = correlate(first, second, halo, cosine, sine, acc[...], blocks)
    keep[...] = total[:, :256]
    send[...] = total[:, 256:].astype(jnp.bfloat16)


def run_chunk(kernel, q, first_hot, second_hot, halo, cosine, sine, acc, outs):
    slots = first_hot.shape[0]
    bins = halo[0].shape[2]

    def rows(width):
        return pl.BlockSpec((ROWS, width), lambda i: (i, 0))

    def whole(shape):
        return pl.BlockSpec(shape, lambda i: (0,) * len(shape))

    operands = [first_hot, second_hot, *halo, cosine, sine] + ([] if acc is None else [acc])
    in_specs = [rows(128), rows(512)]
    in_specs += [whole(b.shape) for b in halo]
    in_specs += [pl.BlockSpec((bins, LAGS), lambda i: (q, 0)) for _ in range(2)]
    in_specs += [] if acc is None else [rows(512)]
    return pl.pallas_call(
        kernel,
        grid=(slots // ROWS,),
        in_specs=in_specs,
        out_specs=[rows(o.shape[1]) for o in outs],
        out_shape=outs,
        scratch_shapes=[pltpu.VMEM((2, 512, bins), jnp.bfloat16)],
        compiler_params=pltpu.CompilerParams(vmem_limit_bytes=24 << 20),
        cost_estimate=pl.CostEstimate(flops=200_000_000, bytes_accessed=1 << 20, transcendentals=0),
        name="correlate",
    )(*operands)


def choose_kernel(has_later, place, crossed, own, *rest):
    outs = rest[-REACH:]
    if has_later:
        rest[-REACH - 1][...] = rest[0][...]
    for d, out in enumerate(outs):

        @pl.when(place[0] <= d)
        def _():
            out[...] = crossed[...]

        @pl.when(place[0] > d)
        def _():
            out[...] = own[...]


def choose(place, crossed, own, later, after, flops):
    shape = jax.ShapeDtypeStruct(own.shape, own.dtype)
    held = [crossed, own] + ([] if later is None else [later])
    vmem = pl.BlockSpec(memory_space=pltpu.VMEM)
    outs = pl.pallas_call(
        functools.partial(choose_kernel, later is not None),
        in_specs=[pl.BlockSpec(memory_space=pltpu.SMEM)]
        + [vmem] * len(held)
        + [pl.BlockSpec(memory_space=pl.ANY)] * len(after),
        out_specs=[vmem] * (REACH + len(held) - 2),
        out_shape=[shape] * (REACH + len(held) - 2),
        compiler_params=pltpu.CompilerParams(vmem_limit_bytes=16 << 20),
        cost_estimate=pl.CostEstimate(flops=flops, bytes_accessed=1 << 20, transcendentals=0),
        name="choose",
    )(place[None], *held, *after)
    return outs[-REACH:], outs[0]


def split_kernel(keep, received, *outs):
    total = keep[...] + received[...].astype(jnp.float32)
    half = total.shape[0] // 2
    for k, out in enumerate(outs):
        piece = total[:, 64 * k : 64 * k + 64]
        out[...] = jnp.concatenate([piece[:half], piece[half:]], 1).astype(out.dtype)


def route_kernel(hot, keep, one, two, three, out):
    total = keep[...]
    for ref in (one, two, three):
        total = total + ref[...].astype(jnp.float32)
    rows = jnp.concatenate([total[:, :64], total[:, 64:]], 0).astype(jnp.bfloat16)
    for owner in range(32):
        placed = dot(hot[64 * owner : 64 * owner + 64, :], rows)
        out[owner] = jnp.concatenate([placed[:32], placed[32:]], 1).astype(jnp.bfloat16)


def unpack_kernel(routed, out):
    for block in range(32):
        values = routed[block].astype(jnp.float32)
        out[0, block, :32] = values[:, :64]
        out[0, block, 32:] = values[:, 64:]


def call(kernel, out_shape, *operands):
    return pl.pallas_call(
        kernel,
        out_shape=out_shape,
        compiler_params=pltpu.CompilerParams(vmem_limit_bytes=24 << 20),
        name=kernel.__name__,
    )(*operands)


def on_device(spectra, pair_first, pair_second, pair_count, pair_owner):
    windows_all = spectra.shape[0] * lax.axis_size("win")
    bins = spectra.shape[3]
    slots = pair_first.shape[1]
    x_place = lax.axis_index("chan") % N_X
    whitened = jnp.swapaxes(whiten(spectra[0]), 0, 1)
    size = bins // CHUNKS
    own = [whitened[:, :, q * size : (q + 1) * size] for q in range(CHUNKS)]
    crossed = [lax.ppermute(own[q], AXES, CROSS) for q in range(2)]

    first_hot = (pair_first[0][:, None] == jnp.arange(128, dtype=jnp.int32)).astype(jnp.bfloat16)
    second_hot = (pair_second[0][:, None] == jnp.arange(512, dtype=jnp.int32)).astype(jnp.bfloat16)
    owners = pair_owner[0, :, 0]
    onehot = (owners[:, None] == jnp.arange(32, dtype=jnp.int32)[None, :]).astype(jnp.int32)
    order = jnp.arange(slots, dtype=jnp.int32)
    below = (order[None, :] < order[:, None]).astype(jnp.bfloat16)
    before = dot(below, onehot.astype(jnp.bfloat16)).astype(jnp.int32)
    place = owners * 64 + jnp.sum(before * onehot, axis=1)
    place = jnp.where(order < pair_count[0], place, -1)
    place_hot = (place[None, :] == jnp.arange(2048, dtype=jnp.int32)[:, None]).astype(jnp.bfloat16)
    cosine, sine = lag_table(bins, windows_all)

    acc = None
    history = []
    f32 = jnp.float32
    for q in range(CHUNKS):
        after = []
        if q >= 2:
            after += [history[q - 2][d] for d in (1, 2, 3)]
        if q >= 1 and FIRST_DONE:
            after += [history[q - 1][2]]
        later = own[q + 2] if q + 2 < CHUNKS else None
        sources, copied = choose(x_place, crossed[q], own[q], later, after, CHOOSE_COST[q])
        if later is not None:
            crossed.append(lax.ppermute(copied, AXES, CROSS))
        ahead = {d: lax.ppermute(sources[d - 1], AXES, AROUND[d]) for d in (2, 1, 3)}
        history.append(ahead)
        halo = [own[q], ahead[1], ahead[2], ahead[3]]
        operands = (q, first_hot, second_hot, halo, cosine, sine, acc)
        whole = jax.ShapeDtypeStruct((slots, LAGS), f32)
        if q == CHUNKS - 1:
            outs = [
                jax.ShapeDtypeStruct((slots, 256), f32),
                jax.ShapeDtypeStruct((slots, 256), jnp.bfloat16),
            ]
            keep, send = run_chunk(last_kernel, *operands, outs)
        else:
            kernel = first_kernel if q == 0 else next_kernel
            (acc,) = run_chunk(kernel, *operands, [whole])
    received = lax.ppermute(send, AXES, OTHER_CORE)
    packed = (slots // 2, 128)
    pieces = call(
        split_kernel,
        [jax.ShapeDtypeStruct(packed, f32)] + [jax.ShapeDtypeStruct(packed, jnp.bfloat16)] * 3,
        keep,
        received,
    )
    arrived = [lax.ppermute(pieces[k], AXES, OTHER_CHIP[k]) for k in (1, 2, 3)]
    buffer = call(
        route_kernel, jax.ShapeDtypeStruct((32, 32, 128), jnp.bfloat16), place_hot, pieces[0], *arrived
    )
    routed = lax.all_to_all(buffer, "chan", split_axis=0, concat_axis=0, tiled=True)
    return call(unpack_kernel, jax.ShapeDtypeStruct((1, 32, 64, 64), f32), routed)


def solution(mesh):
    in_specs = (
        P("win", "chan", None, None),
        P("chan", None),
        P("chan", None),
        P("chan"),
        P("chan", None, None),
    )
    out_specs = P("chan", None, None, "win")
    return jax.shard_map(
        on_device, mesh=mesh, in_specs=in_specs, out_specs=out_specs, check_vma=False
    )
```

```python
import functools
import math

import jax
import jax.numpy as jnp
from jax import lax
from jax.experimental import pallas as pl
from jax.experimental.pallas import tpu as pltpu
from jax.sharding import PartitionSpec as P

LAGS = 512
REACH = 3
SIZES = (512, 512, 512, 512)
CHUNKS = len(SIZES)
FIRST_DONE = (0, 0, 0, 0)
LAG = (0, 0, 0, 3)
CHOOSE_COST = 5_000_000_000
ROWS = 256
AXES = ("chan", "win")
N_X = 4
N_CORE = 2


def pairs_of(move):
    pairs = []
    for chan in range(32):
        for win in range(8):
            row, x, z, core = chan // N_X, chan % N_X, win // N_CORE, win % N_CORE
            target = move(row, x, z, core)
            if target is not None:
                row, x, z, core = target
                pairs.append((chan * 8 + win, (row * N_X + x) * 8 + z * N_CORE + core))
    return pairs


def to_previous_row(row, x, z, core):
    return (row - 1, x, z, core) if row > 0 and x < REACH else None


CROSS = pairs_of(to_previous_row)
AROUND = {d: pairs_of(lambda row, x, z, core, d=d: (row, (x - d) % N_X, z, core)) for d in (1, 2, 3)}
OTHER_CORE = pairs_of(lambda row, x, z, core: (row, x, z, 1 - core))
OTHER_CHIP = {k: pairs_of(lambda row, x, z, core, k=k: (row, x, z ^ k, core)) for k in (1, 2, 3)}


def lag_table(bins, windows):
    win = lax.axis_index("win")
    z, core = win // N_CORE, win % N_CORE
    column = jnp.arange(LAGS, dtype=jnp.int32)
    half, block, inner = column // 256, column // 64 % 4, column % 64
    lag = ((z ^ block) * N_CORE + (core ^ half)) * 64 + inner - LAGS // 2

    def turns(freq_index):
        phase_index = freq_index[:, None] * lag[None, :] % (2 * bins)
        angles = phase_index.astype(jnp.float32) * (math.pi / bins)
        return jnp.cos(angles), jnp.sin(angles)

    few = 32
    low_cos, low_sin = turns(jnp.arange(few, dtype=jnp.int32))
    high_cos, high_sin = turns(jnp.arange(0, bins, few, dtype=jnp.int32))
    low_cos, low_sin = low_cos[None], low_sin[None]
    high_cos, high_sin = high_cos[:, None], high_sin[:, None]
    weights = jnp.where(jnp.arange(bins, dtype=jnp.int32) == 0, 1.0, 2.0).astype(jnp.float32)
    weights = weights.reshape(bins // few, few, 1) / math.sqrt(bins * windows)
    cosine = weights * (high_cos * low_cos - high_sin * low_sin)
    sine = -weights * (high_sin * low_cos + high_cos * low_sin)
    return [part.astype(jnp.bfloat16).reshape(bins, LAGS) for part in (cosine, sine)]


def whiten(spectra):
    values = spectra.astype(jnp.float32)
    power = jnp.mean(values * values, axis=(1, 2), keepdims=True)
    return (values * lax.rsqrt(power + 1e-06)).astype(jnp.bfloat16)


def dot(a, b):
    return lax.dot_general(a, b, (((1,), (0,)), ((), ())), preferred_element_type=jnp.float32)


def correlate(first_ref, second_ref, halo, cos_ref, sin_ref, acc, blocks):
    @pl.when(pl.program_id(0) == 0)
    def _():
        for d, ref in enumerate(halo):
            blocks[:, 128 * d : 128 * (d + 1)] = ref[...]

    left_hot = first_ref[...]
    right_hot = second_ref[...]
    bins = blocks.shape[2]
    step = bins
    for start in range(0, bins, step):
        at = pl.ds(start, step)
        left = [dot(left_hot, blocks[part, :128, at]) for part in range(2)]
        right = [dot(right_hot, blocks[part, :, at]) for part in range(2)]
        real = (left[0] * right[0] + left[1] * right[1]).astype(jnp.bfloat16)
        imag = (left[1] * right[0] - left[0] * right[1]).astype(jnp.bfloat16)
        part = dot(real, cos_ref[at, :]) + dot(imag, sin_ref[at, :])
        acc = part if acc is None else acc + part
    return acc


def first_kernel(first, second, *rest):
    *halo, cosine, sine, out, blocks = rest
    out[...] = correlate(first, second, halo, cosine, sine, None, blocks)


def next_kernel(first, second, *rest):
    *halo, cosine, sine, acc, out, blocks = rest
    out[...] = correlate(first, second, halo, cosine, sine, acc[...], blocks)


def last_kernel(first, second, *rest):
    *halo, cosine, sine, acc, keep, send, blocks = rest
    total = correlate(first, second, halo, cosine, sine, acc[...], blocks)
    keep[...] = total[:, :256]
    send[...] = total[:, 256:].astype(jnp.bfloat16)


def run_chunk(kernel, q, first_hot, second_hot, halo, cosine, sine, acc, outs):
    slots = first_hot.shape[0]
    bins = halo[0].shape[2]

    def rows(width):
        return pl.BlockSpec((ROWS, width), lambda i: (i, 0))

    def whole(shape):
        return pl.BlockSpec(shape, lambda i: (0,) * len(shape))

    operands = [first_hot, second_hot, *halo, cosine, sine] + ([] if acc is None else [acc])
    in_specs = [rows(128), rows(512)]
    in_specs += [whole(b.shape) for b in halo]
    in_specs += [pl.BlockSpec((bins, LAGS), lambda i: (q, 0)) for _ in range(2)]
    in_specs += [] if acc is None else [rows(512)]
    return pl.pallas_call(
        kernel,
        grid=(slots // ROWS,),
        in_specs=in_specs,
        out_specs=[rows(o.shape[1]) for o in outs],
        out_shape=outs,
        scratch_shapes=[pltpu.VMEM((2, 512, bins), jnp.bfloat16)],
        compiler_params=pltpu.CompilerParams(vmem_limit_bytes=24 << 20),
        cost_estimate=pl.CostEstimate(flops=200_000_000, bytes_accessed=1 << 20, transcendentals=0),
        name="correlate",
    )(*operands)


def choose_kernel(has_later, place, crossed, own, *rest):
    outs = rest[-REACH:]
    if has_later:
        rest[-REACH - 1][...] = rest[0][...]
    for d, out in enumerate(outs):

        @pl.when(place[0] <= d)
        def _():
            out[...] = crossed[...]

        @pl.when(place[0] > d)
        def _():
            out[...] = own[...]


def choose(place, crossed, own, later, after, flops):
    held = [crossed, own] + ([] if later is None else [later])
    shapes = [jax.ShapeDtypeStruct(a.shape, a.dtype) for a in held[2:] + [own] * REACH]
    vmem = pl.BlockSpec(memory_space=pltpu.VMEM)
    outs = pl.pallas_call(
        functools.partial(choose_kernel, later is not None),
        in_specs=[pl.BlockSpec(memory_space=pltpu.SMEM)]
        + [vmem] * len(held)
        + [pl.BlockSpec(memory_space=pl.ANY)] * len(after),
        out_specs=[vmem] * len(shapes),
        out_shape=shapes,
        compiler_params=pltpu.CompilerParams(vmem_limit_bytes=16 << 20),
        cost_estimate=pl.CostEstimate(flops=flops, bytes_accessed=1 << 20, transcendentals=0),
        name="choose",
    )(place[None], *held, *after)
    return outs[-REACH:], outs[0]


def hold_kernel(own, after, out):
    out[...] = own[...]


def hold(own, after):
    vmem = pl.BlockSpec(memory_space=pltpu.VMEM)
    return pl.pallas_call(
        hold_kernel,
        in_specs=[vmem, pl.BlockSpec(memory_space=pl.ANY)],
        out_specs=vmem,
        out_shape=jax.ShapeDtypeStruct(own.shape, own.dtype),
        compiler_params=pltpu.CompilerParams(vmem_limit_bytes=16 << 20),
        cost_estimate=pl.CostEstimate(flops=1_000_000, bytes_accessed=1 << 20, transcendentals=0),
        name="hold",
    )(own, after)


def split_kernel(keep, received, *outs):
    total = keep[...] + received[...].astype(jnp.float32)
    half = total.shape[0] // 2
    for k, out in enumerate(outs):
        piece = total[:, 64 * k : 64 * k + 64]
        out[...] = jnp.concatenate([piece[:half], piece[half:]], 1).astype(out.dtype)


def route_kernel(hot, keep, one, two, three, out):
    total = keep[...]
    for ref in (one, two, three):
        total = total + ref[...].astype(jnp.float32)
    rows = jnp.concatenate([total[:, :64], total[:, 64:]], 0).astype(jnp.bfloat16)
    for owner in range(32):
        placed = dot(hot[64 * owner : 64 * owner + 64, :], rows)
        out[owner] = jnp.concatenate([placed[:32], placed[32:]], 1).astype(jnp.bfloat16)


def unpack_kernel(routed, out):
    for block in range(32):
        values = routed[block].astype(jnp.float32)
        out[0, block, :32] = values[:, :64]
        out[0, block, 32:] = values[:, 64:]


def call(kernel, out_shape, *operands):
    return pl.pallas_call(
        kernel,
        out_shape=out_shape,
        compiler_params=pltpu.CompilerParams(vmem_limit_bytes=24 << 20),
        name=kernel.__name__,
    )(*operands)


def on_device(spectra, pair_first, pair_second, pair_count, pair_owner):
    windows_all = spectra.shape[0] * lax.axis_size("win")
    bins = spectra.shape[3]
    slots = pair_first.shape[1]
    x_place = lax.axis_index("chan") % N_X
    whitened = jnp.swapaxes(whiten(spectra[0]), 0, 1)
    starts = [sum(SIZES[:q]) for q in range(CHUNKS)]
    own = [whitened[:, :, at : at + size] for at, size in zip(starts, SIZES)]
    crossed = [lax.ppermute(own[0], AXES, CROSS)]

    first_hot = (pair_first[0][:, None] == jnp.arange(128, dtype=jnp.int32)).astype(jnp.bfloat16)
    second_hot = (pair_second[0][:, None] == jnp.arange(512, dtype=jnp.int32)).astype(jnp.bfloat16)
    owners = pair_owner[0, :, 0]
    onehot = (owners[:, None] == jnp.arange(32, dtype=jnp.int32)[None, :]).astype(jnp.int32)
    order = jnp.arange(slots, dtype=jnp.int32)
    below = (order[None, :] < order[:, None]).astype(jnp.bfloat16)
    before = dot(below, onehot.astype(jnp.bfloat16)).astype(jnp.int32)
    place = owners * 64 + jnp.sum(before * onehot, axis=1)
    place = jnp.where(order < pair_count[0], place, -1)
    place_hot = (place[None, :] == jnp.arange(2048, dtype=jnp.int32)[:, None]).astype(jnp.bfloat16)
    cosine, sine = lag_table(bins, windows_all)
    crossed.append(lax.ppermute(hold(own[1], cosine), AXES, CROSS))

    acc = None
    history, sums = [], []
    f32 = jnp.float32
    for q in range(CHUNKS):
        after = []
        if q >= 2:
            after += [history[q - 2][d] for d in (1, 2, 3)]
        if LAG[q]:
            after.append(sums[q - LAG[q]])
        if q >= 1:
            after += [history[q - 1][d] for d in (2, 1, 3)[: FIRST_DONE[q]]]
        later = own[q + 2] if q + 2 < CHUNKS else None
        sources, copied = choose(x_place, crossed[q], own[q], later, after, CHOOSE_COST)
        if later is not None:
            crossed.append(lax.ppermute(copied, AXES, CROSS))
        ahead = {d: lax.ppermute(sources[d - 1], AXES, AROUND[d]) for d in (2, 1, 3)}
        history.append(ahead)
        halo = [own[q], ahead[1], ahead[2], ahead[3]]
        operands = (q, first_hot, second_hot, halo, cosine, sine, acc)
        whole = jax.ShapeDtypeStruct((slots, LAGS), f32)
        if q == CHUNKS - 1:
            outs = [
                jax.ShapeDtypeStruct((slots, 256), f32),
                jax.ShapeDtypeStruct((slots, 256), jnp.bfloat16),
            ]
            keep, send = run_chunk(last_kernel, *operands, outs)
        else:
            kernel = first_kernel if q == 0 else next_kernel
            (acc,) = run_chunk(kernel, *operands, [whole])
            sums.append(acc)
    received = lax.ppermute(send, AXES, OTHER_CORE)
    packed = (slots // 2, 128)
    pieces = call(
        split_kernel,
        [jax.ShapeDtypeStruct(packed, f32)] + [jax.ShapeDtypeStruct(packed, jnp.bfloat16)] * 3,
        keep,
        received,
    )
    arrived = {k: lax.ppermute(pieces[k], AXES, OTHER_CHIP[k]) for k in (3, 2, 1)}
    buffer = call(
        route_kernel, jax.ShapeDtypeStruct((32, 32, 128), jnp.bfloat16), place_hot, pieces[0], *(arrived[k] for k in (1, 2, 3))
    )
    routed = lax.all_to_all(buffer, "chan", split_axis=0, concat_axis=0, tiled=True)
    return call(unpack_kernel, jax.ShapeDtypeStruct((1, 32, 64, 64), f32), routed)


def solution(mesh):
    in_specs = (
        P("win", "chan", None, None),
        P("chan", None),
        P("chan", None),
        P("chan"),
        P("chan", None, None),
    )
    out_specs = P("chan", None, None, "win")
    return jax.shard_map(
        on_device, mesh=mesh, in_specs=in_specs, out_specs=out_specs, check_vma=False
    )
```

```python
import functools
import math

import jax
import jax.numpy as jnp
from jax import lax
from jax.experimental import pallas as pl
from jax.experimental.pallas import tpu as pltpu
from jax.sharding import PartitionSpec as P

LAGS = 512
REACH = 3
SIZES = (512, 512, 512, 512)
CHUNKS = len(SIZES)
LAG = (0, 0, 0, 3)
CHOOSE_COST = 5_000_000_000
ROWS = 256
AXES = ("chan", "win")
N_X = 4
N_CORE = 2


def pairs_of(move):
    pairs = []
    for chan in range(32):
        for win in range(8):
            row, x, z, core = chan // N_X, chan % N_X, win // N_CORE, win % N_CORE
            target = move(row, x, z, core)
            if target is not None:
                row, x, z, core = target
                pairs.append((chan * 8 + win, (row * N_X + x) * 8 + z * N_CORE + core))
    return pairs


def to_previous_row(row, x, z, core):
    return (row - 1, x, z, core) if row > 0 and x < REACH else None


CROSS = pairs_of(to_previous_row)
AROUND = {d: pairs_of(lambda row, x, z, core, d=d: (row, (x - d) % N_X, z, core)) for d in (1, 2, 3)}
OTHER_CORE = pairs_of(lambda row, x, z, core: (row, x, z, 1 - core))
OTHER_CHIP = {k: pairs_of(lambda row, x, z, core, k=k: (row, x, z ^ k, core)) for k in (1, 2, 3)}


def lag_table(bins, windows):
    win = lax.axis_index("win")
    z, core = win // N_CORE, win % N_CORE
    column = jnp.arange(LAGS, dtype=jnp.int32)
    half, block, inner = column // 256, column // 64 % 4, column % 64
    lag = ((z ^ block) * N_CORE + (core ^ half)) * 64 + inner - LAGS // 2

    def turns(freq_index):
        phase_index = freq_index[:, None] * lag[None, :] % (2 * bins)
        angles = phase_index.astype(jnp.float32) * (math.pi / bins)
        return jnp.cos(angles), jnp.sin(angles)

    few = 32
    low_cos, low_sin = turns(jnp.arange(few, dtype=jnp.int32))
    high_cos, high_sin = turns(jnp.arange(0, bins, few, dtype=jnp.int32))
    low_cos, low_sin = low_cos[None], low_sin[None]
    high_cos, high_sin = high_cos[:, None], high_sin[:, None]
    weights = jnp.where(jnp.arange(bins, dtype=jnp.int32) == 0, 1.0, 2.0).astype(jnp.float32)
    weights = weights.reshape(bins // few, few, 1) / math.sqrt(bins * windows)
    cosine = weights * (high_cos * low_cos - high_sin * low_sin)
    sine = -weights * (high_sin * low_cos + high_cos * low_sin)
    return [part.astype(jnp.bfloat16).reshape(bins, LAGS) for part in (cosine, sine)]


def whitening_scale(spectra):
    values = spectra.astype(jnp.float32)
    return lax.rsqrt(jnp.mean(values * values, axis=(1, 2)) + 1e-06)


def scale_rows(scale, bins):
    pieces = []
    for _ in range(3):
        pieces.append(scale.astype(jnp.bfloat16))
        scale = scale - pieces[-1].astype(jnp.float32)
    return jnp.pad(jnp.stack(pieces), ((0, 13), (0, bins - scale.shape[0])))


def dot(a, b):
    return lax.dot_general(a, b, (((1,), (0,)), ((), ())), preferred_element_type=jnp.float32)


def correlate(first_ref, second_ref, halo, cos_ref, sin_ref, acc, blocks):
    @pl.when(pl.program_id(0) == 0)
    def _():
        for d, ref in enumerate(halo):
            blocks[:, 128 * d : 128 * (d + 1)] = ref[:, :128]

    left_hot = first_ref[...]
    right_hot = second_ref[...]
    bins = blocks.shape[2]
    step = bins
    for start in range(0, bins, step):
        at = pl.ds(start, step)
        left = [dot(left_hot, blocks[part, :128, at]) for part in range(2)]
        right = [dot(right_hot, blocks[part, :, at]) for part in range(2)]
        real = (left[0] * right[0] + left[1] * right[1]).astype(jnp.bfloat16)
        imag = (left[1] * right[0] - left[0] * right[1]).astype(jnp.bfloat16)
        part = dot(real, cos_ref[at, :]) + dot(imag, sin_ref[at, :])
        acc = part if acc is None else acc + part
    return acc


def slot_scale(hot, carriers):
    total = jnp.zeros((hot.shape[0], 128), jnp.float32)
    for d, ref in enumerate(carriers):
        pieces = ref[0, 128:144, :128].astype(jnp.float32)
        scale = pieces[0:1] + pieces[1:2] + pieces[2:3]
        total = total + hot[:, 128 * d : 128 * (d + 1)].astype(jnp.float32) * scale
    return jnp.sum(total, axis=1, keepdims=True)


def first_kernel(first, second, *rest):
    halo, (cosine, sine), carriers, (out, blocks) = rest[:4], rest[4:6], rest[6:10], rest[10:]
    total = correlate(first, second, halo, cosine, sine, None, blocks)
    out[...] = total * (slot_scale(first, carriers[:1]) * slot_scale(second, carriers))


def next_kernel(first, second, *rest):
    *halo, cosine, sine, acc, out, blocks = rest
    out[...] = correlate(first, second, halo, cosine, sine, acc[...], blocks)


def last_kernel(first, second, *rest):
    *halo, cosine, sine, acc, keep, send, blocks = rest
    total = correlate(first, second, halo, cosine, sine, acc[...], blocks)
    keep[...] = total[:, :256]
    send[...] = total[:, 256:].astype(jnp.bfloat16)


def run_chunk(kernel, q, first_hot, second_hot, halo, cosine, sine, acc, carriers, outs):
    slots = first_hot.shape[0]
    bins = halo[0].shape[2]

    def rows(width):
        return pl.BlockSpec((ROWS, width), lambda i: (i, 0))

    def whole(shape):
        return pl.BlockSpec(shape, lambda i: (0,) * len(shape))

    operands = [first_hot, second_hot, *halo, cosine, sine, *carriers] + ([] if acc is None else [acc])
    in_specs = [rows(128), rows(512)]
    in_specs += [whole(b.shape) for b in halo]
    in_specs += [pl.BlockSpec((bins, LAGS), lambda i: (q, 0)) for _ in range(2)]
    in_specs += [whole(c.shape) for c in carriers]
    in_specs += [] if acc is None else [rows(512)]
    return pl.pallas_call(
        kernel,
        grid=(slots // ROWS,),
        in_specs=in_specs,
        out_specs=[rows(o.shape[1]) for o in outs],
        out_shape=outs,
        scratch_shapes=[pltpu.VMEM((2, 512, bins), jnp.bfloat16)],
        compiler_params=pltpu.CompilerParams(vmem_limit_bytes=24 << 20),
        cost_estimate=pl.CostEstimate(flops=200_000_000, bytes_accessed=1 << 20, transcendentals=0),
        name="correlate",
    )(*operands)


def choose_kernel(has_later, place, crossed, own, *rest):
    outs = rest[-REACH:]
    if has_later:
        rest[-REACH - 1][...] = rest[0][...]
    for d, out in enumerate(outs):

        @pl.when(place[0] <= d)
        def _():
            out[...] = crossed[...]

        @pl.when(place[0] > d)
        def _():
            out[...] = own[...]


def choose(place, crossed, own, later, after, flops):
    held = [crossed, own] + ([] if later is None else [later])
    shapes = [jax.ShapeDtypeStruct(a.shape, a.dtype) for a in held[2:] + [own] * REACH]
    vmem = pl.BlockSpec(memory_space=pltpu.VMEM)
    outs = pl.pallas_call(
        functools.partial(choose_kernel, later is not None),
        in_specs=[pl.BlockSpec(memory_space=pltpu.SMEM)]
        + [vmem] * len(held)
        + [pl.BlockSpec(memory_space=pl.ANY)] * len(after),
        out_specs=[vmem] * len(shapes),
        out_shape=shapes,
        compiler_params=pltpu.CompilerParams(vmem_limit_bytes=16 << 20),
        cost_estimate=pl.CostEstimate(flops=flops, bytes_accessed=1 << 20, transcendentals=0),
        name="choose",
    )(place[None], *held, *after)
    return outs[-REACH:], outs[0]


def hold_kernel(own, after, out):
    out[...] = own[...]


def hold(own, after):
    vmem = pl.BlockSpec(memory_space=pltpu.VMEM)
    return pl.pallas_call(
        hold_kernel,
        in_specs=[vmem, pl.BlockSpec(memory_space=pl.ANY)],
        out_specs=vmem,
        out_shape=jax.ShapeDtypeStruct(own.shape, own.dtype),
        compiler_params=pltpu.CompilerParams(vmem_limit_bytes=16 << 20),
        cost_estimate=pl.CostEstimate(flops=1_000_000, bytes_accessed=1 << 20, transcendentals=0),
        name="hold",
    )(own, after)


def part_kernel(apart, out):
    out[...] = apart[...]


def first_part(apart, bins):
    shape = (2, 128, bins)
    return pl.pallas_call(
        part_kernel,
        grid=(1,),
        in_specs=[pl.BlockSpec(shape, lambda i: (0, 0, 0))],
        out_specs=pl.BlockSpec(shape, lambda i: (0, 0, 0)),
        out_shape=jax.ShapeDtypeStruct(shape, apart.dtype),
        compiler_params=pltpu.CompilerParams(vmem_limit_bytes=16 << 20),
        name="first_part",
    )(apart)


def split_kernel(keep, received, *outs):
    total = keep[...] + received[...].astype(jnp.float32)
    half = total.shape[0] // 2
    for k, out in enumerate(outs):
        piece = total[:, 64 * k : 64 * k + 64]
        out[...] = jnp.concatenate([piece[:half], piece[half:]], 1).astype(out.dtype)


def route_kernel(hot, keep, one, two, three, out):
    total = keep[...]
    for ref in (one, two, three):
        total = total + ref[...].astype(jnp.float32)
    rows = jnp.concatenate([total[:, :64], total[:, 64:]], 0).astype(jnp.bfloat16)
    for owner in range(32):
        placed = dot(hot[64 * owner : 64 * owner + 64, :], rows)
        out[owner] = jnp.concatenate([placed[:32], placed[32:]], 1).astype(jnp.bfloat16)


def unpack_kernel(routed, out):
    for block in range(32):
        values = routed[block].astype(jnp.float32)
        out[0, block, :32] = values[:, :64]
        out[0, block, 32:] = values[:, 64:]


def call(kernel, out_shape, *operands):
    return pl.pallas_call(
        kernel,
        out_shape=out_shape,
        compiler_params=pltpu.CompilerParams(vmem_limit_bytes=24 << 20),
        name=kernel.__name__,
    )(*operands)


def on_device(spectra, pair_first, pair_second, pair_count, pair_owner):
    windows_all = spectra.shape[0] * lax.axis_size("win")
    bins = spectra.shape[3]
    slots = pair_first.shape[1]
    x_place = lax.axis_index("chan") % N_X
    apart = jnp.swapaxes(spectra[0], 0, 1)
    starts = [sum(SIZES[:q]) for q in range(CHUNKS)]
    own = [apart[:, :, at : at + size] for at, size in zip(starts, SIZES)]
    own[0] = first_part(apart, SIZES[0])
    crossed = [lax.ppermute(own[0], AXES, CROSS)]
    scale = whitening_scale(hold(spectra, own[0])[0])
    for q in range(1, CHUNKS):
        own[q] = (own[q].astype(jnp.float32) * scale[None, :, None]).astype(jnp.bfloat16)
    extra = scale_rows(scale, SIZES[1])
    own[1] = jnp.concatenate([own[1], jnp.stack([extra, jnp.zeros_like(extra)])], 1)

    pair_first, pair_second = (hold(p, crossed[0]) for p in (pair_first, pair_second))
    first_hot = (pair_first[0][:, None] == jnp.arange(128, dtype=jnp.int32)).astype(jnp.bfloat16)
    second_hot = (pair_second[0][:, None] == jnp.arange(512, dtype=jnp.int32)).astype(jnp.bfloat16)
    owners = pair_owner[0, :, 0]
    onehot = (owners[:, None] == jnp.arange(32, dtype=jnp.int32)[None, :]).astype(jnp.int32)
    order = jnp.arange(slots, dtype=jnp.int32)
    below = (order[None, :] < order[:, None]).astype(jnp.bfloat16)
    before = dot(below, onehot.astype(jnp.bfloat16)).astype(jnp.int32)
    place = owners * 64 + jnp.sum(before * onehot, axis=1)
    place = jnp.where(order < pair_count[0], place, -1)
    place_hot = (place[None, :] == jnp.arange(2048, dtype=jnp.int32)[:, None]).astype(jnp.bfloat16)
    cosine, sine = lag_table(bins, windows_all)
    crossed.append(lax.ppermute(hold(own[1], cosine), AXES, CROSS))

    f32 = jnp.float32
    whole = jax.ShapeDtypeStruct((slots, LAGS), f32)
    ends = [jax.ShapeDtypeStruct((slots, 256), t) for t in (f32, jnp.bfloat16)]
    halos, sums = [], []

    def add_up(q):
        kernel = first_kernel if q == 0 else last_kernel if q == CHUNKS - 1 else next_kernel
        acc = sums[-1] if q else None
        carriers = [] if q else halos[1]
        outs = ends if q == CHUNKS - 1 else [whole]
        return run_chunk(
            kernel, q, first_hot, second_hot, halos[q], cosine, sine, acc, carriers, outs
        )

    for q in range(CHUNKS):
        after = []
        if q >= 2:
            after += halos[q - 2][1:]
        if LAG[q]:
            after.append(sums[q - LAG[q]])
        later = own[q + 2] if q + 2 < CHUNKS else None
        sources, copied = choose(x_place, crossed[q], own[q], later, after, CHOOSE_COST)
        if later is not None:
            crossed.append(lax.ppermute(copied, AXES, CROSS))
        ahead = {d: lax.ppermute(sources[d - 1], AXES, AROUND[d]) for d in (2, 1, 3)}
        halos.append([own[q], ahead[1], ahead[2], ahead[3]])
        if q:
            sums += add_up(q - 1)
    keep, send = add_up(CHUNKS - 1)
    received = lax.ppermute(send, AXES, OTHER_CORE)
    packed = (slots // 2, 128)
    pieces = call(
        split_kernel,
        [jax.ShapeDtypeStruct(packed, f32)] + [jax.ShapeDtypeStruct(packed, jnp.bfloat16)] * 3,
        keep,
        received,
    )
    arrived = {k: lax.ppermute(pieces[k], AXES, OTHER_CHIP[k]) for k in (3, 2, 1)}
    buffer = call(
        route_kernel, jax.ShapeDtypeStruct((32, 32, 128), jnp.bfloat16), place_hot, pieces[0], *(arrived[k] for k in (1, 2, 3))
    )
    routed = lax.all_to_all(buffer, "chan", split_axis=0, concat_axis=0, tiled=True)
    return call(unpack_kernel, jax.ShapeDtypeStruct((1, 32, 64, 64), f32), routed)


def solution(mesh):
    in_specs = (
        P("win", "chan", None, None),
        P("chan", None),
        P("chan", None),
        P("chan"),
        P("chan", None, None),
    )
    out_specs = P("chan", None, None, "win")
    return jax.shard_map(
        on_device, mesh=mesh, in_specs=in_specs, out_specs=out_specs, check_vma=False
    )
```

```python
import functools
import math

import jax
import jax.numpy as jnp
from jax import lax
from jax.experimental import pallas as pl
from jax.experimental.pallas import tpu as pltpu
from jax.sharding import PartitionSpec as P

LAGS = 512
REACH = 3
SIZES = (512, 512, 512, 512)
CHUNKS = len(SIZES)
LAG = (0, 0, 0, 3)
CHOOSE_COST = 5_000_000_000
ROWS = 1024
AXES = ("chan", "win")
N_X = 4
N_CORE = 2


def pairs_of(move):
    pairs = []
    for chan in range(32):
        for win in range(8):
            row, x, z, core = chan // N_X, chan % N_X, win // N_CORE, win % N_CORE
            target = move(row, x, z, core)
            if target is not None:
                row, x, z, core = target
                pairs.append((chan * 8 + win, (row * N_X + x) * 8 + z * N_CORE + core))
    return pairs


def to_previous_row(row, x, z, core):
    return (row - 1, x, z, core) if row > 0 and x < REACH else None


CROSS = pairs_of(to_previous_row)
AROUND = {d: pairs_of(lambda row, x, z, core, d=d: (row, (x - d) % N_X, z, core)) for d in (1, 2, 3)}
OTHER_CORE = pairs_of(lambda row, x, z, core: (row, x, z, 1 - core))
OTHER_CHIP = {k: pairs_of(lambda row, x, z, core, k=k: (row, x, z ^ k, core)) for k in (1, 2, 3)}


def lag_table(bins, windows):
    win = lax.axis_index("win")
    z, core = win // N_CORE, win % N_CORE
    column = jnp.arange(LAGS, dtype=jnp.int32)
    half, block, inner = column // 256, column // 64 % 4, column % 64
    lag = ((z ^ block) * N_CORE + (core ^ half)) * 64 + inner - LAGS // 2

    def turns(freq_index):
        phase_index = freq_index[:, None] * lag[None, :] % (2 * bins)
        angles = phase_index.astype(jnp.float32) * (math.pi / bins)
        return jnp.cos(angles), jnp.sin(angles)

    few = 32
    low_cos, low_sin = turns(jnp.arange(few, dtype=jnp.int32))
    high_cos, high_sin = turns(jnp.arange(0, bins, few, dtype=jnp.int32))
    low_cos, low_sin = low_cos[None], low_sin[None]
    high_cos, high_sin = high_cos[:, None], high_sin[:, None]
    weights = jnp.where(jnp.arange(bins, dtype=jnp.int32) == 0, 1.0, 2.0).astype(jnp.float32)
    weights = weights.reshape(bins // few, few, 1) / math.sqrt(bins * windows)
    cosine = weights * (high_cos * low_cos - high_sin * low_sin)
    sine = -weights * (high_sin * low_cos + high_cos * low_sin)
    return [part.astype(jnp.bfloat16).reshape(bins, LAGS) for part in (cosine, sine)]


def whitening_scale(spectra):
    values = spectra.astype(jnp.float32)
    return lax.rsqrt(jnp.mean(values * values, axis=(1, 2)) + 1e-06)


def scale_rows(scale, bins):
    pieces = []
    for _ in range(3):
        pieces.append(scale.astype(jnp.bfloat16))
        scale = scale - pieces[-1].astype(jnp.float32)
    return jnp.pad(jnp.stack(pieces), ((0, 13), (0, bins - scale.shape[0])))


def dot(a, b):
    return lax.dot_general(a, b, (((1,), (0,)), ((), ())), preferred_element_type=jnp.float32)


def correlate(first_ref, second_ref, halo, cos_ref, sin_ref, acc, blocks):
    @pl.when(pl.program_id(0) == 0)
    def _():
        for d, ref in enumerate(halo):
            blocks[:, 128 * d : 128 * (d + 1)] = ref[:, :128]

    left_hot = first_ref[...]
    right_hot = second_ref[...]
    bins = blocks.shape[2]
    step = 256
    for start in range(0, bins, step):
        at = pl.ds(start, step)
        left = [dot(left_hot, blocks[part, :128, at]) for part in range(2)]
        right = [dot(right_hot, blocks[part, :, at]) for part in range(2)]
        real = (left[0] * right[0] + left[1] * right[1]).astype(jnp.bfloat16)
        imag = (left[1] * right[0] - left[0] * right[1]).astype(jnp.bfloat16)
        part = dot(real, cos_ref[at, :]) + dot(imag, sin_ref[at, :])
        acc = part if acc is None else acc + part
    return acc


def slot_scale(hot, carriers):
    total = jnp.zeros((hot.shape[0], 128), jnp.float32)
    for d, ref in enumerate(carriers):
        pieces = ref[0, 128:144, :128].astype(jnp.float32)
        scale = pieces[0:1] + pieces[1:2] + pieces[2:3]
        total = total + hot[:, 128 * d : 128 * (d + 1)].astype(jnp.float32) * scale
    return jnp.sum(total, axis=1, keepdims=True)


def first_kernel(first, second, *rest):
    halo, (cosine, sine), carriers, (out, blocks) = rest[:4], rest[4:6], rest[6:10], rest[10:]
    total = correlate(first, second, halo, cosine, sine, None, blocks)
    out[...] = total * (slot_scale(first, carriers[:1]) * slot_scale(second, carriers))


def next_kernel(first, second, *rest):
    *halo, cosine, sine, acc, out, blocks = rest
    out[...] = correlate(first, second, halo, cosine, sine, acc[...], blocks)


def last_kernel(first, second, *rest):
    *halo, cosine, sine, acc, keep, send, blocks = rest
    total = correlate(first, second, halo, cosine, sine, acc[...], blocks)
    keep[...] = total[:, :256]
    send[...] = total[:, 256:].astype(jnp.bfloat16)


def run_chunk(kernel, q, first_hot, second_hot, halo, cosine, sine, acc, carriers, outs):
    slots = first_hot.shape[0]
    bins = halo[0].shape[2]

    def rows(width):
        return pl.BlockSpec((ROWS, width), lambda i: (i, 0))

    def whole(shape):
        return pl.BlockSpec(shape, lambda i: (0,) * len(shape))

    operands = [first_hot, second_hot, *halo, cosine, sine, *carriers] + ([] if acc is None else [acc])
    in_specs = [rows(128), rows(512)]
    in_specs += [whole(b.shape) for b in halo]
    in_specs += [pl.BlockSpec((bins, LAGS), lambda i: (q, 0)) for _ in range(2)]
    in_specs += [whole(c.shape) for c in carriers]
    in_specs += [] if acc is None else [rows(512)]
    return pl.pallas_call(
        kernel,
        grid=(slots // ROWS,),
        in_specs=in_specs,
        out_specs=[rows(o.shape[1]) for o in outs],
        out_shape=outs,
        scratch_shapes=[pltpu.VMEM((2, 512, bins), jnp.bfloat16)],
        compiler_params=pltpu.CompilerParams(vmem_limit_bytes=24 << 20),
        cost_estimate=pl.CostEstimate(flops=200_000_000, bytes_accessed=1 << 20, transcendentals=0),
        name="correlate",
    )(*operands)


def choose_kernel(has_later, place, crossed, own, *rest):
    outs = rest[-REACH:]
    if has_later:
        rest[-REACH - 1][...] = rest[0][...]
    for d, out in enumerate(outs):

        @pl.when(place[0] <= d)
        def _():
            out[...] = crossed[...]

        @pl.when(place[0] > d)
        def _():
            out[...] = own[...]


def choose(place, crossed, own, later, after, flops):
    held = [crossed, own] + ([] if later is None else [later])
    shapes = [jax.ShapeDtypeStruct(a.shape, a.dtype) for a in held[2:] + [own] * REACH]
    vmem = pl.BlockSpec(memory_space=pltpu.VMEM)
    outs = pl.pallas_call(
        functools.partial(choose_kernel, later is not None),
        in_specs=[pl.BlockSpec(memory_space=pltpu.SMEM)]
        + [vmem] * len(held)
        + [pl.BlockSpec(memory_space=pl.ANY)] * len(after),
        out_specs=[vmem] * len(shapes),
        out_shape=shapes,
        compiler_params=pltpu.CompilerParams(vmem_limit_bytes=16 << 20),
        cost_estimate=pl.CostEstimate(flops=flops, bytes_accessed=1 << 20, transcendentals=0),
        name="choose",
    )(place[None], *held, *after)
    return outs[-REACH:], outs[0]


def hold_kernel(own, after, out):
    out[...] = own[...]


def hold(own, after):
    vmem = pl.BlockSpec(memory_space=pltpu.VMEM)
    return pl.pallas_call(
        hold_kernel,
        in_specs=[vmem, pl.BlockSpec(memory_space=pl.ANY)],
        out_specs=vmem,
        out_shape=jax.ShapeDtypeStruct(own.shape, own.dtype),
        compiler_params=pltpu.CompilerParams(vmem_limit_bytes=16 << 20),
        cost_estimate=pl.CostEstimate(flops=1_000_000, bytes_accessed=1 << 20, transcendentals=0),
        name="hold",
    )(own, after)


def part_kernel(apart, out):
    out[...] = apart[...]


def first_part(apart, bins):
    shape = (2, 128, bins)
    return pl.pallas_call(
        part_kernel,
        grid=(1,),
        in_specs=[pl.BlockSpec(shape, lambda i: (0, 0, 0))],
        out_specs=pl.BlockSpec(shape, lambda i: (0, 0, 0)),
        out_shape=jax.ShapeDtypeStruct(shape, apart.dtype),
        compiler_params=pltpu.CompilerParams(vmem_limit_bytes=16 << 20),
        name="first_part",
    )(apart)


def split_kernel(keep, received, *outs):
    total = keep[...] + received[...].astype(jnp.float32)
    half = total.shape[0] // 2
    for k, out in enumerate(outs):
        piece = total[:, 64 * k : 64 * k + 64]
        out[...] = jnp.concatenate([piece[:half], piece[half:]], 1).astype(out.dtype)


def route_kernel(hot, keep, one, two, three, out):
    total = keep[...]
    for ref in (one, two, three):
        total = total + ref[...].astype(jnp.float32)
    rows = jnp.concatenate([total[:, :64], total[:, 64:]], 0).astype(jnp.bfloat16)
    for owner in range(32):
        placed = dot(hot[64 * owner : 64 * owner + 64, :], rows)
        out[owner] = jnp.concatenate([placed[:32], placed[32:]], 1).astype(jnp.bfloat16)


def unpack_kernel(routed, out):
    for block in range(32):
        values = routed[block].astype(jnp.float32)
        out[0, block, :32] = values[:, :64]
        out[0, block, 32:] = values[:, 64:]


def call(kernel, out_shape, *operands):
    return pl.pallas_call(
        kernel,
        out_shape=out_shape,
        compiler_params=pltpu.CompilerParams(vmem_limit_bytes=24 << 20),
        name=kernel.__name__,
    )(*operands)


def on_device(spectra, pair_first, pair_second, pair_count, pair_owner):
    windows_all = spectra.shape[0] * lax.axis_size("win")
    bins = spectra.shape[3]
    slots = pair_first.shape[1]
    x_place = lax.axis_index("chan") % N_X
    apart = jnp.swapaxes(spectra[0], 0, 1)
    starts = [sum(SIZES[:q]) for q in range(CHUNKS)]
    own = [apart[:, :, at : at + size] for at, size in zip(starts, SIZES)]
    own[0] = first_part(apart, SIZES[0])
    crossed = [lax.ppermute(own[0], AXES, CROSS)]
    scale = whitening_scale(hold(spectra, own[0])[0])
    for q in range(1, CHUNKS):
        own[q] = (own[q].astype(jnp.float32) * scale[None, :, None]).astype(jnp.bfloat16)
    extra = scale_rows(scale, SIZES[1])
    own[1] = jnp.concatenate([own[1], jnp.stack([extra, jnp.zeros_like(extra)])], 1)

    pair_first, pair_second = (hold(p, crossed[0]) for p in (pair_first, pair_second))
    first_hot = (pair_first[0][:, None] == jnp.arange(128, dtype=jnp.int32)).astype(jnp.bfloat16)
    second_hot = (pair_second[0][:, None] == jnp.arange(512, dtype=jnp.int32)).astype(jnp.bfloat16)
    owners = pair_owner[0, :, 0]
    onehot = (owners[:, None] == jnp.arange(32, dtype=jnp.int32)[None, :]).astype(jnp.int32)
    order = jnp.arange(slots, dtype=jnp.int32)
    below = (order[None, :] < order[:, None]).astype(jnp.bfloat16)
    before = dot(below, onehot.astype(jnp.bfloat16)).astype(jnp.int32)
    place = owners * 64 + jnp.sum(before * onehot, axis=1)
    place = jnp.where(order < pair_count[0], place, -1)
    place_hot = (place[None, :] == jnp.arange(2048, dtype=jnp.int32)[:, None]).astype(jnp.bfloat16)
    cosine, sine = lag_table(bins, windows_all)
    crossed.append(lax.ppermute(hold(own[1], cosine), AXES, CROSS))

    f32 = jnp.float32
    whole = jax.ShapeDtypeStruct((slots, LAGS), f32)
    ends = [jax.ShapeDtypeStruct((slots, 256), t) for t in (f32, jnp.bfloat16)]
    halos, sums = [], []

    def add_up(q):
        kernel = first_kernel if q == 0 else last_kernel if q == CHUNKS - 1 else next_kernel
        acc = sums[-1] if q else None
        carriers = [] if q else halos[1]
        outs = ends if q == CHUNKS - 1 else [whole]
        return run_chunk(
            kernel, q, first_hot, second_hot, halos[q], cosine, sine, acc, carriers, outs
        )

    for q in range(CHUNKS):
        after = []
        if q >= 2:
            after += halos[q - 2][1:]
        if LAG[q]:
            after.append(sums[q - LAG[q]])
        later = own[q + 2] if q + 2 < CHUNKS else None
        sources, copied = choose(x_place, crossed[q], own[q], later, after, CHOOSE_COST)
        if later is not None:
            crossed.append(lax.ppermute(copied, AXES, CROSS))
        ahead = {d: lax.ppermute(sources[d - 1], AXES, AROUND[d]) for d in (2, 1, 3)}
        halos.append([own[q], ahead[1], ahead[2], ahead[3]])
        if q:
            sums += add_up(q - 1)
    keep, send = add_up(CHUNKS - 1)
    received = lax.ppermute(send, AXES, OTHER_CORE)
    packed = (slots // 2, 128)
    pieces = call(
        split_kernel,
        [jax.ShapeDtypeStruct(packed, f32)] + [jax.ShapeDtypeStruct(packed, jnp.bfloat16)] * 3,
        keep,
        received,
    )
    arrived = {k: lax.ppermute(pieces[k], AXES, OTHER_CHIP[k]) for k in (3, 2, 1)}
    buffer = call(
        route_kernel, jax.ShapeDtypeStruct((32, 32, 128), jnp.bfloat16), place_hot, pieces[0], *(arrived[k] for k in (1, 2, 3))
    )
    routed = lax.all_to_all(buffer, "chan", split_axis=0, concat_axis=0, tiled=True)
    return call(unpack_kernel, jax.ShapeDtypeStruct((1, 32, 64, 64), f32), routed)


def solution(mesh):
    in_specs = (
        P("win", "chan", None, None),
        P("chan", None),
        P("chan", None),
        P("chan"),
        P("chan", None, None),
    )
    out_specs = P("chan", None, None, "win")
    return jax.shard_map(
        on_device, mesh=mesh, in_specs=in_specs, out_specs=out_specs, check_vma=False
    )
```

```python
import functools
import math

import jax
import jax.numpy as jnp
from jax import lax
from jax.experimental import pallas as pl
from jax.experimental.pallas import tpu as pltpu
from jax.sharding import PartitionSpec as P

LAGS = 512
REACH = 3
SIZES = (512, 512, 512, 512)
CHUNKS = len(SIZES)
LAG = (0, 0, 0, 3)
CHOOSE_COST = 5_000_000_000
ROWS = 1024
AXES = ("chan", "win")
N_X = 4
N_CORE = 2


def pairs_of(move):
    pairs = []
    for chan in range(32):
        for win in range(8):
            row, x, z, core = chan // N_X, chan % N_X, win // N_CORE, win % N_CORE
            target = move(row, x, z, core)
            if target is not None:
                row, x, z, core = target
                pairs.append((chan * 8 + win, (row * N_X + x) * 8 + z * N_CORE + core))
    return pairs


def to_previous_row(row, x, z, core):
    return (row - 1, x, z, core) if row > 0 and x < REACH else None


CROSS = pairs_of(to_previous_row)
AROUND = {d: pairs_of(lambda row, x, z, core, d=d: (row, (x - d) % N_X, z, core)) for d in (1, 2, 3)}
OTHER_CORE = pairs_of(lambda row, x, z, core: (row, x, z, 1 - core))
OTHER_CHIP = {k: pairs_of(lambda row, x, z, core, k=k: (row, x, z ^ k, core)) for k in (1, 2, 3)}


def lag_table(bins, windows):
    win = lax.axis_index("win")
    z, core = win // N_CORE, win % N_CORE
    column = jnp.arange(LAGS, dtype=jnp.int32)
    half, block, inner = column // 256, column // 64 % 4, column % 64
    lag = ((z ^ block) * N_CORE + (core ^ half)) * 64 + inner - LAGS // 2

    def turns(freq_index):
        phase_index = freq_index[:, None] * lag[None, :] % (2 * bins)
        angles = phase_index.astype(jnp.float32) * (math.pi / bins)
        return jnp.cos(angles), jnp.sin(angles)

    few = 32
    low_cos, low_sin = turns(jnp.arange(few, dtype=jnp.int32))
    high_cos, high_sin = turns(jnp.arange(0, bins, few, dtype=jnp.int32))
    low_cos, low_sin = low_cos[None], low_sin[None]
    high_cos, high_sin = high_cos[:, None], high_sin[:, None]
    weights = jnp.where(jnp.arange(bins, dtype=jnp.int32) == 0, 1.0, 2.0).astype(jnp.float32)
    weights = weights.reshape(bins // few, few, 1) / math.sqrt(bins * windows)
    cosine = weights * (high_cos * low_cos - high_sin * low_sin)
    sine = -weights * (high_sin * low_cos + high_cos * low_sin)
    return [part.astype(jnp.bfloat16).reshape(bins, LAGS) for part in (cosine, sine)]


def whitening_scale(spectra):
    values = spectra.astype(jnp.float32)
    return lax.rsqrt(jnp.mean(values * values, axis=(1, 2)) + 1e-06)


def scale_rows(scale, bins):
    pieces = []
    for _ in range(3):
        pieces.append(scale.astype(jnp.bfloat16))
        scale = scale - pieces[-1].astype(jnp.float32)
    return jnp.pad(jnp.stack(pieces), ((0, 13), (0, bins - scale.shape[0])))


def dot(a, b):
    return lax.dot_general(a, b, (((1,), (0,)), ((), ())), preferred_element_type=jnp.float32)


def correlate(first_ref, second_ref, halo, cos_ref, sin_ref, acc, blocks):
    @pl.when(pl.program_id(0) == 0)
    def _():
        for d, ref in enumerate(halo):
            blocks[:, 128 * d : 128 * (d + 1)] = ref[:, :128]

    left_hot = first_ref[...]
    right_hot = second_ref[...]
    bins = blocks.shape[2]
    step = 256
    for start in range(0, bins, step):
        at = pl.ds(start, step)
        left = [dot(left_hot, blocks[part, :128, at]) for part in range(2)]
        right = [dot(right_hot, blocks[part, :, at]) for part in range(2)]
        real = (left[0] * right[0] + left[1] * right[1]).astype(jnp.bfloat16)
        imag = (left[1] * right[0] - left[0] * right[1]).astype(jnp.bfloat16)
        part = dot(real, cos_ref[at, :]) + dot(imag, sin_ref[at, :])
        acc = part if acc is None else acc + part
    return acc


def slot_scale(hot, carriers):
    total = jnp.zeros((hot.shape[0], 128), jnp.float32)
    for d, ref in enumerate(carriers):
        pieces = ref[0, 128:144, :128].astype(jnp.float32)
        scale = pieces[0:1] + pieces[1:2] + pieces[2:3]
        total = total + hot[:, 128 * d : 128 * (d + 1)].astype(jnp.float32) * scale
    return jnp.sum(total, axis=1, keepdims=True)


def first_kernel(first, second, *rest):
    halo, (cosine, sine), carriers, (out, blocks) = rest[:4], rest[4:6], rest[6:10], rest[10:]
    total = correlate(first, second, halo, cosine, sine, None, blocks)
    out[...] = total * (slot_scale(first, carriers[:1]) * slot_scale(second, carriers))


def next_kernel(first, second, *rest):
    *halo, cosine, sine, acc, out, blocks = rest
    out[...] = correlate(first, second, halo, cosine, sine, acc[...], blocks)


def last_kernel(first, second, *rest):
    *halo, cosine, sine, acc, keep, send, blocks = rest
    total = correlate(first, second, halo, cosine, sine, acc[...], blocks)
    keep[...] = total[:, :256]
    send[...] = total[:, 256:].astype(jnp.bfloat16)


def run_chunk(kernel, q, first_hot, second_hot, halo, cosine, sine, acc, carriers, outs):
    slots = first_hot.shape[0]
    bins = halo[0].shape[2]

    def rows(width):
        return pl.BlockSpec((ROWS, width), lambda i: (i, 0))

    def whole(shape):
        return pl.BlockSpec(shape, lambda i: (0,) * len(shape))

    operands = [first_hot, second_hot, *halo, cosine, sine, *carriers] + ([] if acc is None else [acc])
    in_specs = [rows(128), rows(512)]
    in_specs += [whole(b.shape) for b in halo]
    in_specs += [pl.BlockSpec((bins, LAGS), lambda i: (q, 0)) for _ in range(2)]
    in_specs += [whole(c.shape) for c in carriers]
    in_specs += [] if acc is None else [rows(512)]
    return pl.pallas_call(
        kernel,
        grid=(slots // ROWS,),
        in_specs=in_specs,
        out_specs=[rows(o.shape[1]) for o in outs],
        out_shape=outs,
        scratch_shapes=[pltpu.VMEM((2, 512, bins), jnp.bfloat16)],
        compiler_params=pltpu.CompilerParams(vmem_limit_bytes=24 << 20),
        cost_estimate=pl.CostEstimate(flops=200_000_000, bytes_accessed=1 << 20, transcendentals=0),
        name="correlate",
    )(*operands)


def choose_kernel(has_later, place, crossed, own, *rest):
    outs = rest[-REACH:]
    if has_later:
        rest[-REACH - 1][...] = rest[0][...]
    for d, out in enumerate(outs):

        @pl.when(place[0] <= d)
        def _():
            out[...] = crossed[...]

        @pl.when(place[0] > d)
        def _():
            out[...] = own[...]


def choose(place, crossed, own, later, after, flops):
    held = [crossed, own] + ([] if later is None else [later])
    shapes = [jax.ShapeDtypeStruct(a.shape, a.dtype) for a in held[2:] + [own] * REACH]
    vmem = pl.BlockSpec(memory_space=pltpu.VMEM)
    outs = pl.pallas_call(
        functools.partial(choose_kernel, later is not None),
        in_specs=[pl.BlockSpec(memory_space=pltpu.SMEM)]
        + [vmem] * len(held)
        + [pl.BlockSpec(memory_space=pl.ANY)] * len(after),
        out_specs=[vmem] * len(shapes),
        out_shape=shapes,
        compiler_params=pltpu.CompilerParams(vmem_limit_bytes=16 << 20),
        cost_estimate=pl.CostEstimate(flops=flops, bytes_accessed=1 << 20, transcendentals=0),
        name="choose",
    )(place[None], *held, *after)
    return outs[-REACH:], outs[0]


def hold_kernel(own, after, out):
    out[...] = own[...]


def hold(own, after):
    vmem = pl.BlockSpec(memory_space=pltpu.VMEM)
    return pl.pallas_call(
        hold_kernel,
        in_specs=[vmem, pl.BlockSpec(memory_space=pl.ANY)],
        out_specs=vmem,
        out_shape=jax.ShapeDtypeStruct(own.shape, own.dtype),
        compiler_params=pltpu.CompilerParams(vmem_limit_bytes=16 << 20),
        cost_estimate=pl.CostEstimate(flops=1_000_000, bytes_accessed=1 << 20, transcendentals=0),
        name="hold",
    )(own, after)


def part_kernel(apart, out):
    out[...] = apart[...]


def first_part(apart, bins):
    shape = (2, 128, bins)
    return pl.pallas_call(
        part_kernel,
        grid=(1,),
        in_specs=[pl.BlockSpec(shape, lambda i: (0, 0, 0))],
        out_specs=pl.BlockSpec(shape, lambda i: (0, 0, 0)),
        out_shape=jax.ShapeDtypeStruct(shape, apart.dtype),
        compiler_params=pltpu.CompilerParams(vmem_limit_bytes=16 << 20),
        name="first_part",
    )(apart)


def split_kernel(keep, received, *outs):
    total = keep[...] + received[...].astype(jnp.float32)
    half = total.shape[0] // 2
    for k, out in enumerate(outs):
        piece = total[:, 64 * k : 64 * k + 64]
        out[...] = jnp.concatenate([piece[:half], piece[half:]], 1).astype(out.dtype)


def route_kernel(hot, keep, one, two, three, out):
    total = keep[...]
    for ref in (one, two, three):
        total = total + ref[...].astype(jnp.float32)
    rows = jnp.concatenate([total[:, :64], total[:, 64:]], 0).astype(jnp.bfloat16)
    for owner in range(32):
        placed = dot(hot[64 * owner : 64 * owner + 64, :], rows)
        out[owner] = jnp.concatenate([placed[:32], placed[32:]], 1).astype(jnp.bfloat16)


def unpack_kernel(routed, out):
    for block in range(routed.shape[0]):
        values = routed[block].astype(jnp.float32)
        out[0, block, :32] = values[:, :64]
        out[0, block, 32:] = values[:, 64:]


def unpack(routed):
    blocks = 8
    return pl.pallas_call(
        unpack_kernel,
        grid=(routed.shape[0] // blocks,),
        in_specs=[pl.BlockSpec((blocks, 32, 128), lambda i: (i, 0, 0))],
        out_specs=pl.BlockSpec((1, blocks, 64, 64), lambda i: (0, i, 0, 0)),
        out_shape=jax.ShapeDtypeStruct((1, routed.shape[0], 64, 64), jnp.float32),
        compiler_params=pltpu.CompilerParams(vmem_limit_bytes=24 << 20),
        name="unpack",
    )(routed)


def call(kernel, out_shape, *operands):
    return pl.pallas_call(
        kernel,
        out_shape=out_shape,
        compiler_params=pltpu.CompilerParams(vmem_limit_bytes=24 << 20),
        name=kernel.__name__,
    )(*operands)


def on_device(spectra, pair_first, pair_second, pair_count, pair_owner):
    windows_all = spectra.shape[0] * lax.axis_size("win")
    bins = spectra.shape[3]
    slots = pair_first.shape[1]
    x_place = lax.axis_index("chan") % N_X
    apart = jnp.swapaxes(spectra[0], 0, 1)
    starts = [sum(SIZES[:q]) for q in range(CHUNKS)]
    own = [apart[:, :, at : at + size] for at, size in zip(starts, SIZES)]
    own[0] = first_part(apart, SIZES[0])
    crossed = [lax.ppermute(own[0], AXES, CROSS)]
    scale = whitening_scale(hold(spectra, own[0])[0])
    for q in range(1, CHUNKS):
        own[q] = (own[q].astype(jnp.float32) * scale[None, :, None]).astype(jnp.bfloat16)
    extra = scale_rows(scale, SIZES[1])
    own[1] = jnp.concatenate([own[1], jnp.stack([extra, jnp.zeros_like(extra)])], 1)

    pair_first, pair_second = (hold(p, crossed[0]) for p in (pair_first, pair_second))
    first_hot = (pair_first[0][:, None] == jnp.arange(128, dtype=jnp.int32)).astype(jnp.bfloat16)
    second_hot = (pair_second[0][:, None] == jnp.arange(512, dtype=jnp.int32)).astype(jnp.bfloat16)
    owners = pair_owner[0, :, 0]
    onehot = (owners[:, None] == jnp.arange(32, dtype=jnp.int32)[None, :]).astype(jnp.int32)
    order = jnp.arange(slots, dtype=jnp.int32)
    below = (order[None, :] < order[:, None]).astype(jnp.bfloat16)
    before = dot(below, onehot.astype(jnp.bfloat16)).astype(jnp.int32)
    place = owners * 64 + jnp.sum(before * onehot, axis=1)
    place = jnp.where(order < pair_count[0], place, -1)
    place_hot = (place[None, :] == jnp.arange(2048, dtype=jnp.int32)[:, None]).astype(jnp.bfloat16)
    cosine, sine = lag_table(bins, windows_all)
    crossed.append(lax.ppermute(hold(own[1], cosine), AXES, CROSS))

    f32 = jnp.float32
    whole = jax.ShapeDtypeStruct((slots, LAGS), f32)
    ends = [jax.ShapeDtypeStruct((slots, 256), t) for t in (f32, jnp.bfloat16)]
    halos, sums = [], []

    def add_up(q):
        kernel = first_kernel if q == 0 else last_kernel if q == CHUNKS - 1 else next_kernel
        acc = sums[-1] if q else None
        carriers = [] if q else halos[1]
        outs = ends if q == CHUNKS - 1 else [whole]
        return run_chunk(
            kernel, q, first_hot, second_hot, halos[q], cosine, sine, acc, carriers, outs
        )

    for q in range(CHUNKS):
        after = []
        if q >= 2:
            after += halos[q - 2][1:]
        if LAG[q]:
            after.append(sums[q - LAG[q]])
        later = own[q + 2] if q + 2 < CHUNKS else None
        sources, copied = choose(x_place, crossed[q], own[q], later, after, CHOOSE_COST)
        if later is not None:
            crossed.append(lax.ppermute(copied, AXES, CROSS))
        ahead = {d: lax.ppermute(sources[d - 1], AXES, AROUND[d]) for d in (2, 1, 3)}
        halos.append([own[q], ahead[1], ahead[2], ahead[3]])
        if q:
            sums += add_up(q - 1)
    keep, send = add_up(CHUNKS - 1)
    received = lax.ppermute(send, AXES, OTHER_CORE)
    packed = (slots // 2, 128)
    pieces = call(
        split_kernel,
        [jax.ShapeDtypeStruct(packed, f32)] + [jax.ShapeDtypeStruct(packed, jnp.bfloat16)] * 3,
        keep,
        received,
    )
    arrived = {k: lax.ppermute(pieces[k], AXES, OTHER_CHIP[k]) for k in (3, 2, 1)}
    buffer = call(
        route_kernel, jax.ShapeDtypeStruct((32, 32, 128), jnp.bfloat16), place_hot, pieces[0], *(arrived[k] for k in (1, 2, 3))
    )
    routed = lax.all_to_all(buffer, "chan", split_axis=0, concat_axis=0, tiled=True)
    return unpack(routed)


def solution(mesh):
    in_specs = (
        P("win", "chan", None, None),
        P("chan", None),
        P("chan", None),
        P("chan"),
        P("chan", None, None),
    )
    out_specs = P("chan", None, None, "win")
    return jax.shard_map(
        on_device, mesh=mesh, in_specs=in_specs, out_specs=out_specs, check_vma=False
    )
```
